256 devices in a mesh: dp: 16 (over y, x), seq: 16 (over z, core).
Axes of the slice: x: 4, y: 4, z: 8, core: 2. Of those that a mesh axis runs over, the one named last changes fastest.
Arguments:
- queries: bfloat16 [32768, 8192], P(('dp', 'seq')), parts along dimension 0, may hold values from -7 to 7
- key_rows: bfloat16 [32768, 1024], P(('dp', 'seq')), parts along dimension 0, may hold values from -5 to 5
- value_rows: bfloat16 [32768, 1024], P(('dp', 'seq')), parts along dimension 0, may hold values from -6 to 6
- outputs: bfloat16 [32768, 8192], P(('dp', 'seq')), parts along dimension 0, may hold values from -3 to 3
- out_grads: bfloat16 [32768, 8192], P(('dp', 'seq')), parts along dimension 0, may hold values from -1.5 to 1.5
- log_normalizer: float32 [32768, 64], P(('dp', 'seq')), parts along dimension 0, may hold values from -30 to 40, as said below
- doc_starts: int32 [128], P('dp'), parts along dimension 0, may hold values from 0 to 2047, as said below
- doc_weights: float32 [128], P('dp'), parts along dimension 0, may hold values from 0.25 to 2.5
Outputs:
- query_grads: bfloat16 [32768, 8192], P(('dp', 'seq')), parts along dimension 0
- key_grads: bfloat16 [32768, 1024], P(('dp', 'seq')), parts along dimension 0
- value_grads: bfloat16 [32768, 1024], P(('dp', 'seq')), parts along dimension 0
The draws below stay inside these ranges and needn't reach their ends.
There are 16 independent parts, one for each index of `dp`. The reference program is written for one: setup_inputs(seed, part) draws one part's arguments, and reference() takes and returns one part's arrays. A program takes and returns all parts, laid end to end along the dimension named above; each array names one. Nothing has to cross between parts.
Inputs may be any that keep to these rules, and one draw needn't show every extreme that they name: `doc_starts`: 8 documents in order: starts rise from 0, each document runs to the next start or to the end of the window, is 1 to 512 tokens long, and one is exactly 512 long. `log_normalizer`: the log of the sum of exp(scores) over the allowed keys of each token and head.
All inputs are finite; a program needn't handle non-finite values.
Results may differ from the reference program's by a relative error of at most 0.0049.
Values may be sent and summed in bfloat16 or wider, within the bound.
A program may use at most 128 MiB of HBM per device.

```python
import math
import jax
import jax.numpy as jnp
from jax import lax

HEADS = 64
KVH = 8
HD = 128
DOCS = 8
TOKENS = 2048
MAXDOC = 512
GQA = 8


def doc_table(key):
    key = jax.random.fold_in(key, 101)
    place_key, jitter_key = jax.random.split(key)
    remainder = TOKENS - MAXDOC
    others = DOCS - 1
    spacing = remainder // others
    half_gap = (spacing - 1) // 2
    jitter = jax.random.randint(jitter_key, (others - 1,), -half_gap, half_gap + 1, dtype=jnp.int32)
    inner_cuts = jnp.arange(1, others, dtype=jnp.int32) * spacing + jitter
    bounds = jnp.concatenate([jnp.zeros((1,), jnp.int32), inner_cuts, jnp.full((1,), remainder, jnp.int32)])
    other_lengths = bounds[1:] - bounds[:-1]
    big_slot = jax.random.randint(place_key, (), 0, DOCS, dtype=jnp.int32)
    slot_index = jnp.arange(DOCS, dtype=jnp.int32)
    source = jnp.clip(slot_index - (slot_index > big_slot).astype(jnp.int32), 0, others - 1)
    lengths = jnp.where(slot_index == big_slot, MAXDOC, other_lengths[source]).astype(jnp.int32)
    return (jnp.cumsum(lengths) - lengths).astype(jnp.int32)


def query_table(key):
    key = jax.random.fold_in(key, 102)
    return jnp.clip(jax.random.normal(key, (TOKENS, HEADS * HD), jnp.float32), -4.5, 4.5)


def key_table(key):
    key = jax.random.fold_in(key, 103)
    return jnp.clip(jax.random.normal(key, (TOKENS, KVH * HD), jnp.float32), -4.5, 4.5)


def draw_queries(key, part):
    return query_table(key).astype(jnp.bfloat16)


def draw_key_rows(key, part):
    return key_table(key).astype(jnp.bfloat16)


def draw_doc_starts(key, part):
    return doc_table(key)


def draw_log_normalizer(key, part):
    query_wide = query_table(key).astype(jnp.bfloat16).astype(jnp.float32)
    key_wide = key_table(key).astype(jnp.bfloat16).astype(jnp.float32)
    starts = doc_table(key)
    positions = jnp.arange(TOKENS, dtype=jnp.int32)
    doc_of = jnp.sum((positions[:, None] >= starts[None, :]).astype(jnp.int32), axis=1) - 1
    allowed = (doc_of[:, None] == doc_of[None, :]) & (positions[None, :] <= positions[:, None])
    query_groups = query_wide.reshape(TOKENS, KVH, GQA, HD).transpose(1, 0, 2, 3)
    key_groups = key_wide.reshape(TOKENS, KVH, HD).transpose(1, 0, 2)

    def single_group(operands):
        query_part, key_part = operands
        scores = jnp.einsum('qhd,kd->hqk', query_part, key_part) * HD ** (-0.5)
        masked = jnp.where(allowed[None], scores, -1e+30)
        return jax.nn.logsumexp(masked, axis=-1)
    result = lax.map(single_group, (query_groups, key_groups))
    return result.transpose(2, 0, 1).reshape(TOKENS, HEADS).astype(jnp.float32)


def level_of(own_key, dims, pieces, low, largest):
    def one(axis_at, parts):
        heights = jax.random.uniform(jax.random.fold_in(jax.random.fold_in(own_key, 6), axis_at), (parts,), jnp.float32, low / len(pieces), largest / len(pieces))
        return jnp.repeat(jnp.exp(heights), dims[axis_at] // parts).reshape((-1,) + (1,) * (len(dims) - axis_at - 1))

    gain = one(*pieces[0])
    for cut in pieces[1:]:
        gain = gain * one(*cut)
    return gain


def centred(rng, dims, scale, bound, shards=(), kind=jnp.bfloat16):
    loudness = level_of(rng, dims, shards, -0.22, 0.18) if shards else 1.0
    values = jax.random.normal(rng, dims, jnp.float32) * scale * loudness
    return jnp.minimum(jnp.maximum(values, -bound), bound).astype(kind)


def setup_inputs(seed: int = 0, part: int = 0) -> dict:
    seeds = jax.random.split(jax.random.key(seed), 9)
    part_keys = jax.random.split(jax.random.fold_in(seeds[8], part), 9)
    queries = draw_queries(jax.random.fold_in(jax.random.fold_in(seeds[8], part), 71), part)
    key_rows = draw_key_rows(jax.random.fold_in(jax.random.fold_in(seeds[8], part), 71), part)
    value_rows = centred(part_keys[2], (TOKENS, KVH * HD), 1.0, 6.0, ((0, 16),))
    outputs = centred(part_keys[3], (TOKENS, HEADS * HD), 0.5, 3.0, ((0, 16),))
    out_grads = centred(part_keys[4], (TOKENS, HEADS * HD), 0.25, 1.5, ((0, 16),))
    log_normalizer = draw_log_normalizer(jax.random.fold_in(jax.random.fold_in(seeds[8], part), 71), part)
    doc_starts = draw_doc_starts(jax.random.fold_in(jax.random.fold_in(seeds[8], part), 71), part)
    doc_weights = jnp.clip(jnp.exp(jax.random.uniform(part_keys[7], (DOCS,), jnp.float32, math.log(0.25), math.log(2.5))), 0.25, 2.5)
    return {"queries": queries, "key_rows": key_rows, "value_rows": value_rows, "outputs": outputs, "out_grads": out_grads, "log_normalizer": log_normalizer, "doc_starts": doc_starts, "doc_weights": doc_weights}


def reference(queries, key_rows, value_rows, outputs, out_grads, log_normalizer, doc_starts, doc_weights):
    positions = jnp.arange(TOKENS, dtype=jnp.int32)
    doc_of = jnp.sum((positions[:, None] >= doc_starts[None, :]).astype(jnp.int32), axis=1) - 1
    member = doc_of[:, None] == jnp.arange(DOCS, dtype=jnp.int32)[None, :]
    row_weight = jnp.sum(jnp.where(member, doc_weights[None, :], jnp.zeros((), doc_weights.dtype)), axis=1)
    allowed = (doc_of[:, None] == doc_of[None, :]) & (positions[None, :] <= positions[:, None])
    score_scale = HD ** -0.5
    product = out_grads.astype(jnp.float32) * outputs.astype(jnp.float32)
    row_delta = jnp.sum(product.reshape(TOKENS, HEADS, HD), axis=-1)
    query_groups = queries.reshape(TOKENS, KVH, GQA, HD).transpose(1, 0, 2, 3)
    grad_groups = out_grads.reshape(TOKENS, KVH, GQA, HD).transpose(1, 0, 2, 3)
    key_groups = key_rows.reshape(TOKENS, KVH, HD).transpose(1, 0, 2)
    value_groups = value_rows.reshape(TOKENS, KVH, HD).transpose(1, 0, 2)
    norm_groups = log_normalizer.reshape(TOKENS, KVH, GQA).transpose(1, 2, 0)
    delta_groups = row_delta.reshape(TOKENS, KVH, GQA).transpose(1, 2, 0)

    def single_group(operands):
        query_part, key_part, value_part, grad_part, norm_part, delta_part = operands
        query_wide = query_part.astype(jnp.float32)
        key_wide = key_part.astype(jnp.float32)
        value_wide = value_part.astype(jnp.float32)
        grad_wide = grad_part.astype(jnp.float32)
        scores = jnp.einsum("qhd,kd->hqk", query_wide, key_wide) * score_scale
        probs = jnp.where(allowed[None], jnp.exp(scores - norm_part[:, :, None]), jnp.zeros((), scores.dtype))
        mean_score = jnp.sum(probs * scores, axis=-1)
        prob_grads = jnp.einsum("qhd,kd->hqk", grad_wide, value_wide)
        score_grads = probs * (prob_grads - delta_part[:, :, None] - row_weight[None, :, None] * (scores - mean_score[:, :, None]))
        score_low = lax.optimization_barrier(score_grads.astype(jnp.bfloat16)).astype(jnp.float32)
        probs_low = lax.optimization_barrier(probs.astype(jnp.bfloat16)).astype(jnp.float32)
        query_out = (jnp.einsum("hqk,kd->qhd", score_low, key_wide) * score_scale).astype(jnp.bfloat16)
        key_out = (jnp.einsum("hqk,qhd->kd", score_low, query_wide) * score_scale).astype(jnp.bfloat16)
        value_out = jnp.einsum("hqk,qhd->kd", probs_low, grad_wide).astype(jnp.bfloat16)
        return query_out, key_out, value_out

    query_out, key_out, value_out = lax.map(single_group, (query_groups, key_groups, value_groups, grad_groups, norm_groups, delta_groups))
    query_grads = query_out.transpose(1, 0, 2, 3).reshape(TOKENS, HEADS * HD)
    key_grads = key_out.transpose(1, 0, 2).reshape(TOKENS, KVH * HD)
    value_grads = value_out.transpose(1, 0, 2).reshape(TOKENS, KVH * HD)
    return (query_grads, key_grads, value_grads)
```

```python
import functools
import math

import jax
import jax.numpy as jnp
from jax import lax
from jax.experimental import pallas as pl
from jax.experimental.pallas import tpu as pltpu
from jax.sharding import PartitionSpec as P

HEADS = 64
KVH = 8
HD = 128
GQA = HEADS // KVH
GW = GQA * HD
SCALE = HD ** (-0.5)
LOG2E = math.log2(math.e)
NT = (((1,), (1,)), ((), ()))
f32 = jnp.float32
bf16 = jnp.bfloat16

NEAR_AHEAD = 3


def kernel(
    starts, weights, q_hbm, do_hbm, o_hbm, k_ref, v_ref, ln_ref,
    dq_hbm, dk_ref, dv_ref,
    kv, q_s, do_s, o_s, bias, wcol, norm_t, p_s, ds_s, dq_s,
    pe_out, pe_in, own, a4_out, a4_in, f_out, f_in,
    in_sem, dq_sem, near_sem, far_sem, e1_sem, e3_sem, x1_sem, x3_sem, a4_sem, f_sem,
):
    tok = k_ref.shape[0]
    docs = starts.shape[0]
    me = lax.axis_index("seq")
    n = lax.axis_size("seq")
    up = {"seq": lax.rem(me + 2, n)}
    down = {"seq": lax.rem(me + n - 2, n)}
    parity = lax.rem(me, 2)
    mate = {"seq": me + 1 - 2 * parity}
    even = parity == 0

    def load(g, i):
        src = (q_hbm, do_hbm, o_hbm)[i]
        dst = (q_s, do_s, o_s)[i]
        return pltpu.make_async_copy(
            src.at[:, pl.ds(pl.multiple_of(g * GW, GW), GW)], dst.at[g], in_sem.at[i, g]
        )

    def dq_out(g):
        return pltpu.make_async_copy(
            dq_s.at[g], dq_hbm.at[:, pl.ds(pl.multiple_of(g * GW, GW), GW)], dq_sem.at[g]
        )

    def remote(src, dst, sem, g, where):
        return pltpu.make_async_remote_copy(
            src_ref=src, dst_ref=dst, send_sem=sem.at[0, g], recv_sem=sem.at[1, g],
            device_id=where, device_id_type=pl.DeviceIdType.MESH,
        )

    def rows(g, start):
        return kv.at[g, pl.ds(start, tok), :]

    def near(g):
        return remote(rows(g, 4 * tok), rows(g, 2 * tok), near_sem, g, up)

    def far(g):
        return remote(rows(g, 2 * tok), rows(g, 0), far_sem, g, up)

    def mate1(g):
        src = pl.multiple_of((4 - 2 * parity) * tok, tok)
        return remote(rows(g, src), rows(g, 3 * tok), e1_sem, g, mate)

    def mate3(g):
        src = pl.multiple_of((2 - 2 * parity) * tok, tok)
        return remote(rows(g, src), rows(g, tok), e3_sem, g, mate)

    def back1(g):
        return remote(pe_out.at[g, 1], pe_in.at[g, 1], x1_sem, g, mate)

    def back3(g):
        return remote(pe_out.at[g, 0], pe_in.at[g, 0], x3_sem, g, mate)

    def back_far(g):
        return remote(a4_out.at[g], a4_in.at[g], a4_sem, g, down)

    def back_near(g):
        return remote(f_out.at[g], f_in.at[g], f_sem, g, down)

    def each(lo, hi, fn):
        def step(i, carry):
            fn(i)
            return carry
        lax.fori_loop(lo, hi, step, 0)

    for i in range(3):
        each(0, KVH, lambda g: load(g, i).start())

    barrier = pltpu.get_barrier_semaphore()
    for where in (up, down, mate):
        pl.semaphore_signal(barrier, inc=1, device_id=where, device_id_type=pl.DeviceIdType.MESH)
    for g in range(KVH):
        kv[g, 4 * tok :, 0:HD] = k_ref[:, g * HD : (g + 1) * HD]
        kv[g, 4 * tok :, HD:] = v_ref[:, g * HD : (g + 1) * HD]
    pl.semaphore_wait(barrier, 3)

    for g in range(NEAR_AHEAD):
        near(g).start()

    base = me * tok
    pos_lane = lax.broadcasted_iota(jnp.int32, (8, tok), 1) + base
    pos_row = lax.broadcasted_iota(jnp.int32, (tok, HD), 0) + base
    start_row = jnp.zeros((8, tok), jnp.int32)
    w_row = jnp.zeros((8, tok), f32)
    w_col = jnp.zeros((tok, HD), f32)
    for d in range(docs):
        start_row = jnp.where(pos_lane >= starts[d], starts[d], start_row)
        w_row = jnp.where(pos_lane >= starts[d], weights[d], w_row)
        w_col = jnp.where(pos_row >= starts[d], weights[d], w_col)
    wcol[...] = w_col * (-SCALE)
    w_row = w_row[0:1] * SCALE
    key_pos = lax.broadcasted_iota(jnp.int32, (5 * tok, tok), 0) + (base - 4 * tok)
    query_pos = lax.broadcasted_iota(jnp.int32, (5 * tok, tok), 1) + base
    allowed = (key_pos >= start_row[0:1]) & (key_pos <= query_pos)
    bias[...] = jnp.where(allowed, 0.0, -1e30).astype(f32)
    norm_t[...] = ln_ref[...].T * LOG2E
    lane = lax.broadcasted_iota(jnp.int32, (tok, HD), 1)

    def arrive_near(g):
        near(g).wait_recv()
        far(g).start()
        mate1(g).start()

    def arrive_far(g):
        far(g).wait_recv()
        mate3(g).start()

    def arrive_mate(g):
        mate1(g).wait_recv()
        mate3(g).wait_recv()

    def compute(g):
        kvw = kv[g]
        delta = jnp.zeros((tok, HD), f32)
        for h in range(GQA):
            cols = slice(h * HD, (h + 1) * HD)
            prod = do_s[g, :, cols].astype(f32) * o_s[g, :, cols].astype(f32)
            delta = jnp.where(lane == h, jnp.sum(prod, axis=1, keepdims=True), delta)
        delta = delta.T[0:GQA]
        norm = norm_t[pl.ds(pl.multiple_of(g * GQA, GQA), GQA), :]
        mask = bias[...]
        for h in range(GQA):
            cols = slice(h * HD, (h + 1) * HD)
            q = q_s[g, :, cols]
            do = do_s[g, :, cols]
            wq = (q.astype(f32) * wcol[...]).astype(bf16)
            s = lax.dot_general(kvw[:, :HD], q, NT, preferred_element_type=f32)
            gs = lax.dot_general(
                kvw, jnp.concatenate([wq, do], 1), NT, preferred_element_type=f32
            )
            p = jnp.exp2(s * (SCALE * LOG2E) + mask - norm[h : h + 1])
            mean = jnp.sum(p * s, axis=0, keepdims=True)
            ds = p * (gs + (w_row * mean - delta[h : h + 1]))
            p_s[:, cols] = p.astype(bf16)
            ds_s[:, cols] = ds.astype(bf16)
        q_all = jnp.concatenate([q_s[g, :, h * HD : (h + 1) * HD] for h in range(GQA)], 0)
        do_all = jnp.concatenate([do_s[g, :, h * HD : (h + 1) * HD] for h in range(GQA)], 0)
        dk = jnp.dot(ds_s[...], q_all, preferred_element_type=f32) * SCALE
        dv = jnp.dot(p_s[...], do_all, preferred_element_type=f32)
        for part, block in enumerate((dk, dv)):
            cols = slice(part * HD, (part + 1) * HD)
            own[g, 2, :, cols] = block[0:tok]
            pe_out[g, 0, :, cols] = block[tok : 2 * tok].astype(bf16)
            own[g, 1, :, cols] = block[2 * tok : 3 * tok]
            pe_out[g, 1, :, cols] = block[3 * tok : 4 * tok].astype(bf16)
            own[g, 0, :, cols] = block[4 * tok :]
        back1(g).start()
        back3(g).start()
        dq_t = jnp.dot(kvw[:, :HD].T, ds_s[...], preferred_element_type=f32) * SCALE
        for h in range(GQA):
            cols = slice(h * HD, (h + 1) * HD)
            dq_s[g, :, cols] = dq_t[:, cols].T.astype(bf16)
        dq_out(g).start()

    def grads_mate(g):
        back1(g).wait_recv()
        back3(g).wait_recv()
        one = pe_in[g, 1].astype(f32)
        three = pe_in[g, 0].astype(f32)
        zero = jnp.zeros_like(one)
        a4_out[g] = (own[g, 2] + jnp.where(even, zero, three)).astype(bf16)
        back_far(g).start()
        own[g, 1] = own[g, 1] + jnp.where(even, three, one)
        own[g, 0] = own[g, 0] + jnp.where(even, one, zero)

    def grads_far(g):
        back_far(g).wait_recv()
        f_out[g] = (own[g, 1] + a4_in[g].astype(f32)).astype(bf16)
        back_near(g).start()

    def grads_near(g):
        back_near(g).wait_recv()
        total = (own[g, 0] + f_in[g].astype(f32)).astype(bf16)
        cols = pl.ds(pl.multiple_of(g * HD, HD), HD)
        dk_ref[:, cols] = total[:, :HD]
        dv_ref[:, cols] = total[:, HD:]

    arrive_near(0)
    near(NEAR_AHEAD).start()
    arrive_near(1)
    near(NEAR_AHEAD + 1).start()
    arrive_far(0)

    def step(g, carry):
        @pl.when(g + 2 < KVH)
        def _():
            arrive_near(g + 2)

        @pl.when(g + 2 + NEAR_AHEAD < KVH)
        def _():
            near(g + 2 + NEAR_AHEAD).start()

        @pl.when(g + 1 < KVH)
        def _():
            arrive_far(g + 1)

        arrive_mate(g)
        for i in range(3):
            load(g, i).wait()
        compute(g)

        @pl.when(g >= 1)
        def _():
            grads_mate(g - 1)

        @pl.when(g >= 2)
        def _():
            grads_far(g - 2)

        @pl.when(g >= 3)
        def _():
            grads_near(g - 3)

        return carry

    lax.fori_loop(0, KVH, step, 0)
    grads_mate(KVH - 1)
    grads_far(KVH - 2)
    grads_near(KVH - 3)
    grads_far(KVH - 1)
    grads_near(KVH - 2)
    grads_near(KVH - 1)

    def finish(g, carry):
        for copy in (near, far, mate1, mate3, back1, back3, back_far, back_near):
            copy(g).wait_send()
        dq_out(g).wait()
        return carry

    lax.fori_loop(0, KVH, finish, 0)


def per_device(
    queries, key_rows, value_rows, outputs, out_grads, log_normalizer, doc_starts, doc_weights
):
    tok = queries.shape[0]
    vmem = pl.BlockSpec(memory_space=pltpu.VMEM)
    smem = pl.BlockSpec(memory_space=pltpu.SMEM)
    hbm = pl.BlockSpec(memory_space=pl.ANY)
    dma = pltpu.SemaphoreType.DMA
    block = (KVH, tok, 2 * HD)
    return pl.pallas_call(
        kernel,
        out_shape=(
            jax.ShapeDtypeStruct(queries.shape, bf16),
            jax.ShapeDtypeStruct(key_rows.shape, bf16),
            jax.ShapeDtypeStruct(value_rows.shape, bf16),
        ),
        in_specs=[smem, smem, hbm, hbm, hbm, vmem, vmem, vmem],
        out_specs=(hbm, vmem, vmem),
        scratch_shapes=[
            pltpu.VMEM((KVH, 5 * tok, 2 * HD), bf16),
            pltpu.VMEM((KVH, tok, GW), bf16),
            pltpu.VMEM((KVH, tok, GW), bf16),
            pltpu.VMEM((KVH, tok, GW), bf16),
            pltpu.VMEM((5 * tok, tok), f32),
            pltpu.VMEM((tok, HD), f32),
            pltpu.VMEM((HEADS, tok), f32),
            pltpu.VMEM((5 * tok, GW), bf16),
            pltpu.VMEM((5 * tok, GW), bf16),
            pltpu.VMEM((KVH, tok, GW), bf16),
            pltpu.VMEM((KVH, 2, tok, 2 * HD), bf16),
            pltpu.VMEM((KVH, 2, tok, 2 * HD), bf16),
            pltpu.VMEM((KVH, 3, tok, 2 * HD), f32),
            pltpu.VMEM(block, bf16),
            pltpu.VMEM(block, bf16),
            pltpu.VMEM(block, bf16),
            pltpu.VMEM(block, bf16),
            dma((3, KVH)),
            dma((KVH,)),
        ]
        + [dma((2, KVH))] * 8,
        compiler_params=pltpu.CompilerParams(
            collective_id=0, has_side_effects=True, vmem_limit_bytes=56 * 1024 * 1024
        ),
        cost_estimate=pl.CostEstimate(
            flops=10 * HEADS * tok * 5 * tok * HD, bytes_accessed=9 * queries.size, transcendentals=0
        ),
    )(doc_starts, doc_weights, queries, out_grads, outputs, key_rows, value_rows, log_normalizer)


def solution(mesh):
    rows = P(("dp", "seq"), None)
    in_specs = (rows, rows, rows, rows, rows, rows, P("dp"), P("dp"))
    return jax.shard_map(
        per_device, mesh=mesh, in_specs=in_specs, out_specs=(rows, rows, rows), check_vma=False
    )
```

```python
import functools
import math

import jax
import jax.numpy as jnp
from jax import lax
from jax.experimental import pallas as pl
from jax.experimental.pallas import tpu as pltpu
from jax.sharding import PartitionSpec as P

HEADS = 64
KVH = 8
HD = 128
GQA = HEADS // KVH
GW = GQA * HD
SCALE = HD ** (-0.5)
LOG2E = math.log2(math.e)
NT = (((1,), (1,)), ((), ()))
VMEM_BYTES = 56 * 1024 * 1024
f32 = jnp.float32
bf16 = jnp.bfloat16

AHEAD_SEND = 7
AHEAD_PASS = 4
AHEAD_PAIR = 2
LAG_PASS = 4
LAG_LAST = 7
STRAIGHT = 2


def kernel(
    starts, weights, q_hbm, do_hbm, o_hbm, k_hbm, v_hbm, norm_hbm,
    dq_ref, dk_ref, dv_ref,
    kv, q_s, do_s, o_s, bias, wcol, norm_t, delta_t, mean_t, p32_s, p_s, ds_s, k_s, v_s, norm_s,
    pair_out, pair_in, own, far_out, far_in, near_out, near_in,
    in_sem, small_sem, near_sem, far_sem, mate_sem, pair_sem, back_far_sem, back_near_sem,
):
    tok = k_hbm.shape[0]
    docs = starts.shape[0]
    units = 2 * KVH
    me = lax.axis_index("seq")
    n = lax.axis_size("seq")
    parity = lax.rem(me, 2)
    even = parity == 0
    up = {"seq": lax.rem(me + 2, n)}
    up_two = {"seq": lax.rem(me + 4, n)}
    down = {"seq": lax.rem(me + n - 2, n)}
    down_two = {"seq": lax.rem(me + n - 4, n)}
    mate = {"seq": me + 1 - 2 * parity}

    def load(g, i):
        src = (q_hbm, do_hbm, o_hbm)[i]
        dst = (q_s, do_s, o_s)[i]
        return pltpu.make_async_copy(
            src.at[:, pl.ds(pl.multiple_of(g * GW, GW), GW)], dst.at[g], in_sem.at[i, g]
        )

    def load_small(i):
        src = (k_hbm, v_hbm, norm_hbm)[i]
        dst = (k_s, v_s, norm_s)[i]
        return pltpu.make_async_copy(src, dst, small_sem.at[i])

    def remote(src, dst, sem, u, where):
        return pltpu.make_async_remote_copy(
            src_ref=src, dst_ref=dst, send_sem=sem.at[0, u], recv_sem=sem.at[1, u],
            device_id=where, device_id_type=pl.DeviceIdType.MESH,
        )

    def rows(u, start, size=1):
        return kv.at[u, pl.ds(start, size * tok), :]

    def near(u):
        return remote(rows(u, 0), rows(u, tok), near_sem, u, up)

    def far(u):
        return remote(rows(u, tok), rows(u, 2 * tok), far_sem, u, up)

    def share(u):
        src = pl.multiple_of(parity * tok, tok)
        return remote(rows(u, src, 2), rows(u, 3 * tok, 2), mate_sem, u, mate)

    def pair(u):
        return remote(pair_out.at[u], pair_in.at[u], pair_sem, u, mate)

    def back_far(u):
        return remote(far_out.at[u], far_in.at[u], back_far_sem, u, down)

    def back_far_two(u):
        return remote(far_out.at[u], far_in.at[u], back_far_sem, u, down_two)

    def back_near(u):
        return remote(near_out.at[u], near_in.at[u], back_near_sem, u, down)

    def each(lo, hi, fn):
        def step(i, carry):
            fn(i)
            return carry
        lax.fori_loop(lo, hi, step, 0)

    barrier = pltpu.get_barrier_semaphore()
    partners = (up, down, mate, up_two, down_two)
    for where in partners:
        pl.semaphore_signal(barrier, inc=1, device_id=where, device_id_type=pl.DeviceIdType.MESH)
    for i in range(3):
        load_small(i).start()
    for i in (1, 2, 0):
        each(0, KVH, lambda g: load(g, i).start())
    load_small(0).wait()
    load_small(1).wait()
    for g in range(KVH):
        kv[2 * g, 0:tok, :] = k_s[:, g * HD : (g + 1) * HD]
        kv[2 * g + 1, 0:tok, :] = v_s[:, g * HD : (g + 1) * HD]
    pl.semaphore_wait(barrier, len(partners))
    for u in range(AHEAD_PASS):
        near(u).start()

    base = me * tok
    pos_lane = lax.broadcasted_iota(jnp.int32, (8, tok), 1) + base
    pos_row = lax.broadcasted_iota(jnp.int32, (tok, HD), 0) + base
    start_row = jnp.zeros((8, tok), jnp.int32)
    w_row = jnp.zeros((8, tok), f32)
    w_col = jnp.zeros((tok, HD), f32)
    for d in range(docs):
        start_row = jnp.where(pos_lane >= starts[d], starts[d], start_row)
        w_row = jnp.where(pos_lane >= starts[d], weights[d], w_row)
        w_col = jnp.where(pos_row >= starts[d], weights[d], w_col)
    wcol[...] = w_col * (-SCALE)
    w_row = w_row[0:1] * SCALE
    query_pos = lax.broadcasted_iota(jnp.int32, (tok, tok), 1) + base
    for i, behind in enumerate((0, 2, 4, 1, 3)):
        key_pos = lax.broadcasted_iota(jnp.int32, (tok, tok), 0) + (base - behind * tok)
        allowed = (key_pos >= start_row[0:1]) & (key_pos <= query_pos)
        bias[i * tok : (i + 1) * tok, :] = jnp.where(allowed, 0.0, -1e30).astype(f32)
    load_small(2).wait()
    norm_t[...] = norm_s[...] * LOG2E
    lane = lax.broadcasted_iota(jnp.int32, (tok, HD), 1)

    def row_deltas(g):
        load(g, 1).wait()
        load(g, 2).wait()
        delta = jnp.zeros((tok, HD), f32)
        for h in range(GQA):
            cols = slice(h * HD, (h + 1) * HD)
            prod = do_s[g, :, cols].astype(f32) * o_s[g, :, cols].astype(f32)
            delta = jnp.where(lane == h, jnp.sum(prod, axis=1, keepdims=True), delta)
        delta_t[pl.ds(pl.multiple_of(g * GQA, GQA), GQA), :] = delta.T[0:GQA]

    each(0, KVH, row_deltas)
    each(0, KVH, lambda g: load(g, 0).wait())

    def pass_on(u):
        near(u).wait_recv()
        far(u).start()

    def give_mate(u):
        far(u).wait_recv()
        share(u).start()

    def put_grad(u, block):
        pair_out[u] = block[3 * tok :].astype(bf16)
        pair(u).start()
        own[u] = block[0 : 3 * tok]

    def stack(ref, g):
        return jnp.concatenate([ref[g, :, h * HD : (h + 1) * HD] for h in range(GQA)], 0)

    def probs_phase(g):
        keys = kv[2 * g]
        norm = norm_t[pl.ds(pl.multiple_of(g * GQA, GQA), GQA), :]
        mask = bias[...]
        for h in range(GQA):
            cols = slice(h * HD, (h + 1) * HD)
            s = lax.dot_general(keys, q_s[g, :, cols], NT, preferred_element_type=f32)
            p = jnp.exp2(s * (SCALE * LOG2E) + mask - norm[h : h + 1])
            mean_t[h : h + 1, :] = jnp.sum(p * s, axis=0, keepdims=True)
            p32_s[:, cols] = p
            p_s[:, cols] = p.astype(bf16)
        put_grad(2 * g, jnp.dot(p_s[...], stack(do_s, g), preferred_element_type=f32))

    def grads_phase(g):
        window = jnp.concatenate([kv[2 * g], kv[2 * g + 1]], 1)
        delta = delta_t[pl.ds(pl.multiple_of(g * GQA, GQA), GQA), :]
        offset = w_row * mean_t[...] - delta
        for h in range(GQA):
            cols = slice(h * HD, (h + 1) * HD)
            wq = (q_s[g, :, cols].astype(f32) * wcol[...]).astype(bf16)
            gs = lax.dot_general(
                window, jnp.concatenate([wq, do_s[g, :, cols]], 1), NT, preferred_element_type=f32
            )
            ds_s[g, :, cols] = (p32_s[:, cols] * (gs + offset[h : h + 1])).astype(bf16)
        put_grad(
            2 * g + 1, jnp.dot(ds_s[g], stack(q_s, g), preferred_element_type=f32) * SCALE
        )

    def query_phase(g):
        dq_t = jnp.dot(kv[2 * g].T, ds_s[g], preferred_element_type=f32) * SCALE
        for h in range(GQA):
            cols = slice(h * HD, (h + 1) * HD)
            dq_ref[g, :, cols] = dq_t[:, cols].T.astype(bf16)

    def grads_mate(u):
        pair(u).wait_recv()
        one = pair_in[u, 0:tok].astype(f32)
        three = pair_in[u, tok:].astype(f32)
        zero = jnp.zeros_like(one)
        far_out[u] = (own[u, 2 * tok :] + jnp.where(even, zero, three)).astype(bf16)
        own[u, 0:tok] = own[u, 0:tok] + jnp.where(even, one, zero)
        return own[u, tok : 2 * tok] + jnp.where(even, three, one)

    def grads_mate_pass(u):
        block = grads_mate(u)
        back_far(u).start()
        own[u, tok : 2 * tok] = block

    def grads_mate_straight(u):
        near_out[u] = grads_mate(u).astype(bf16)
        back_near(u).start()
        back_far_two(u).start()

    def grads_pass(u):
        back_far(u).wait_recv()
        near_out[u] = (own[u, tok : 2 * tok] + far_in[u].astype(f32)).astype(bf16)
        back_near(u).start()

    def grads_last(u):
        back_near(u).wait_recv()
        own[u, 0:tok] = own[u, 0:tok] + near_in[u].astype(f32)

    def grads_last_straight(u):
        back_far_two(u).wait_recv()
        own[u, 0:tok] = own[u, 0:tok] + far_in[u].astype(f32)
        grads_last(u)

    def between(u):
        @pl.when(u + AHEAD_PASS < units)
        def _():
            pass_on(u + AHEAD_PASS)

        @pl.when(u + AHEAD_SEND < units)
        def _():
            near(u + AHEAD_SEND).start()

        @pl.when(u + AHEAD_PAIR < units)
        def _():
            give_mate(u + AHEAD_PAIR)

        @pl.when((u >= 1) & (u - 1 < units - STRAIGHT))
        def _():
            grads_mate_pass(u - 1)

        @pl.when(u - 1 >= units - STRAIGHT)
        def _():
            grads_mate_straight(u - 1)

        @pl.when(u >= LAG_PASS)
        def _():
            grads_pass(u - LAG_PASS)

        @pl.when(u >= LAG_LAST)
        def _():
            grads_last(u - LAG_LAST)

    for u in range(AHEAD_PASS):
        pass_on(u)
        if AHEAD_PASS + u < AHEAD_SEND:
            near(AHEAD_PASS + u).start()
    for u in range(2 * AHEAD_PASS, AHEAD_SEND):
        near(u).start()
    for u in range(AHEAD_PAIR):
        give_mate(u)

    def step(g, carry):
        share(2 * g).wait_recv()
        probs_phase(g)
        between(2 * g)
        share(2 * g + 1).wait_recv()
        grads_phase(g)
        between(2 * g + 1)
        return carry

    lax.fori_loop(0, KVH, step, 0)
    grads_mate_straight(units - 1)
    each(units - LAG_PASS, units - STRAIGHT, grads_pass)
    each(0, KVH, query_phase)
    each(units - LAG_LAST, units - STRAIGHT, grads_last)
    each(units - STRAIGHT, units, grads_last_straight)
    for g in range(KVH):
        cols = slice(g * HD, (g + 1) * HD)
        dv_ref[:, cols] = own[2 * g, 0:tok].astype(bf16)
        dk_ref[:, cols] = own[2 * g + 1, 0:tok].astype(bf16)

    def finish(u):
        for copy in (near, far, share, pair, back_far, back_near):
            copy(u).wait_send()

    each(0, units, finish)


def out_kernel(dq_in, dk_in, dv_in, dq, dk, dv, sems):
    groups = dq_in.shape[0]
    copies = [
        pltpu.make_async_copy(dq_in.at[g], dq.at[:, g * GW : (g + 1) * GW], sems.at[g])
        for g in range(groups)
    ]
    copies.append(pltpu.make_async_copy(dk_in, dk, sems.at[groups]))
    copies.append(pltpu.make_async_copy(dv_in, dv, sems.at[groups + 1]))
    for copy in copies:
        copy.start()
    for copy in copies:
        copy.wait()


def finish_out(dq, dk, dv):
    vmem = pl.BlockSpec(memory_space=pltpu.VMEM)
    hbm = pl.BlockSpec(memory_space=pl.ANY)
    groups, tok, width = dq.shape
    return pl.pallas_call(
        out_kernel,
        out_shape=(
            jax.ShapeDtypeStruct((tok, groups * width), dq.dtype),
            jax.ShapeDtypeStruct(dk.shape, dk.dtype),
            jax.ShapeDtypeStruct(dv.shape, dv.dtype),
        ),
        in_specs=[vmem] * 3,
        out_specs=(hbm,) * 3,
        scratch_shapes=[pltpu.SemaphoreType.DMA((groups + 2,))],
        compiler_params=pltpu.CompilerParams(vmem_limit_bytes=VMEM_BYTES),
    )(dq, dk, dv)


def per_device(
    queries, key_rows, value_rows, outputs, out_grads, log_normalizer, doc_starts, doc_weights
):
    tok = queries.shape[0]
    units = 2 * KVH
    vmem = pl.BlockSpec(memory_space=pltpu.VMEM)
    smem = pl.BlockSpec(memory_space=pltpu.SMEM)
    hbm = pl.BlockSpec(memory_space=pl.ANY)
    dma = pltpu.SemaphoreType.DMA
    heads = pltpu.VMEM((KVH, tok, GW), bf16)
    block = pltpu.VMEM((units, tok, HD), bf16)
    pair = pltpu.VMEM((units, 2 * tok, HD), bf16)
    tile = pltpu.VMEM((5 * tok, GW), bf16)
    out = pl.pallas_call(
        kernel,
        out_shape=(
            pltpu.VMEM((KVH, tok, GW), bf16),
            pltpu.VMEM(key_rows.shape, bf16),
            pltpu.VMEM(value_rows.shape, bf16),
        ),
        in_specs=[smem, smem] + [hbm] * 6,
        out_specs=(vmem,) * 3,
        scratch_shapes=[
            pltpu.VMEM((units, 5 * tok, HD), bf16),
            heads, heads, heads,
            pltpu.VMEM((5 * tok, tok), f32),
            pltpu.VMEM((tok, HD), f32),
            pltpu.VMEM((HEADS, tok), f32),
            pltpu.VMEM((HEADS, tok), f32),
            pltpu.VMEM((GQA, tok), f32),
            pltpu.VMEM((5 * tok, GW), f32),
            tile,
            pltpu.VMEM((KVH, 5 * tok, GW), bf16),
            pltpu.VMEM(key_rows.shape, bf16),
            pltpu.VMEM(value_rows.shape, bf16),
            pltpu.VMEM((HEADS, tok), f32),
            pair, pair,
            pltpu.VMEM((units, 3 * tok, HD), f32),
            block, block, block, block,
            dma((3, KVH)),
            dma((3,)),
        ]
        + [dma((2, units))] * 6,
        compiler_params=pltpu.CompilerParams(
            collective_id=0, has_side_effects=True, vmem_limit_bytes=VMEM_BYTES
        ),
        cost_estimate=pl.CostEstimate(
            flops=10 * HEADS * tok * 5 * tok * HD, bytes_accessed=9 * queries.size, transcendentals=0
        ),
    )(doc_starts, doc_weights, queries, out_grads, outputs, key_rows, value_rows, log_normalizer.T)
    return finish_out(*[pltpu.with_memory_space_constraint(x, pltpu.VMEM) for x in out])


def solution(mesh):
    rows = P(("dp", "seq"), None)
    in_specs = (rows, rows, rows, rows, rows, rows, P("dp"), P("dp"))
    return jax.shard_map(
        per_device, mesh=mesh, in_specs=in_specs, out_specs=(rows, rows, rows), check_vma=False
    )
```

```python
import functools
import math

import jax
import jax.numpy as jnp
from jax import lax
from jax.experimental import pallas as pl
from jax.experimental.pallas import tpu as pltpu
from jax.sharding import PartitionSpec as P

HEADS = 64
KVH = 8
HD = 128
GQA = HEADS // KVH
GW = GQA * HD
SCALE = HD ** (-0.5)
LOG2E = math.log2(math.e)
NT = (((1,), (1,)), ((), ()))
VMEM_BYTES = 56 * 1024 * 1024
f32 = jnp.float32
bf16 = jnp.bfloat16

AHEAD_SEND = 8
AHEAD_PASS = 5
AHEAD_PAIR = 2
LAG_PASS = 4
LAG_LAST = 7
STRAIGHT_FIRST = 0
STRAIGHT_LAST = 1


def kernel(
    starts, weights, q_hbm, do_hbm, o_hbm, k_hbm, v_hbm, norm_hbm,
    dq_ref, dk_ref, dv_ref,
    kv, q_s, do_s, o_s, bias, wcol, norm_t, delta_t, mean_t, p32_s, p_s, ds_s, k_s, v_s, norm_s,
    pair_out, pair_in, own, far_out, far_in, near_out, near_in,
    in_sem, small_sem, near_sem, far_sem, mate_sem, pair_sem, back_far_sem, back_near_sem,
):
    tok = k_hbm.shape[0]
    docs = starts.shape[0]
    units = 2 * KVH
    me = lax.axis_index("seq")
    n = lax.axis_size("seq")
    parity = lax.rem(me, 2)
    even = parity == 0
    up = {"seq": lax.rem(me + 2, n)}
    up_two = {"seq": lax.rem(me + 4, n)}
    down = {"seq": lax.rem(me + n - 2, n)}
    down_two = {"seq": lax.rem(me + n - 4, n)}
    mate = {"seq": me + 1 - 2 * parity}

    def load(g, i):
        src = (q_hbm, do_hbm, o_hbm)[i]
        dst = (q_s, do_s, o_s)[i]
        return pltpu.make_async_copy(
            src.at[:, pl.ds(pl.multiple_of(g * GW, GW), GW)], dst.at[g], in_sem.at[i, g]
        )

    def load_small(i):
        src = (k_hbm, v_hbm, norm_hbm)[i]
        dst = (k_s, v_s, norm_s)[i]
        return pltpu.make_async_copy(src, dst, small_sem.at[i])

    def remote(src, dst, sem, u, where):
        return pltpu.make_async_remote_copy(
            src_ref=src, dst_ref=dst, send_sem=sem.at[0, u], recv_sem=sem.at[1, u],
            device_id=where, device_id_type=pl.DeviceIdType.MESH,
        )

    def rows(u, start, size=1):
        return kv.at[u, pl.ds(start, size * tok), :]

    def near(u):
        return remote(rows(u, 0), rows(u, tok), near_sem, u, up)

    def far(u):
        return remote(rows(u, tok), rows(u, 2 * tok), far_sem, u, up)

    def share(u):
        src = pl.multiple_of(parity * tok, tok)
        return remote(rows(u, src, 2), rows(u, 3 * tok, 2), mate_sem, u, mate)

    def pair(u):
        return remote(pair_out.at[u], pair_in.at[u], pair_sem, u, mate)

    def back_far(u):
        return remote(far_out.at[u], far_in.at[u], back_far_sem, u, down)

    def back_far_two(u):
        return remote(far_out.at[u], far_in.at[u], back_far_sem, u, down_two)

    def back_near(u):
        return remote(near_out.at[u], near_in.at[u], back_near_sem, u, down)

    def each(lo, hi, fn):
        def step(i, carry):
            fn(i)
            return carry
        lax.fori_loop(lo, hi, step, 0)

    barrier = pltpu.get_barrier_semaphore()
    partners = (up, down, mate, up_two, down_two)
    for where in partners:
        pl.semaphore_signal(barrier, inc=1, device_id=where, device_id_type=pl.DeviceIdType.MESH)
    for i in range(3):
        load_small(i).start()
    for i in (1, 2, 0):
        each(0, KVH, lambda g: load(g, i).start())
    load_small(0).wait()
    load_small(1).wait()
    for g in range(KVH):
        kv[2 * g, 0:tok, :] = k_s[:, g * HD : (g + 1) * HD]
        kv[2 * g + 1, 0:tok, :] = v_s[:, g * HD : (g + 1) * HD]
    pl.semaphore_wait(barrier, len(partners))
    for u in range(AHEAD_PASS):
        near(u).start()

    base = me * tok
    pos_lane = lax.broadcasted_iota(jnp.int32, (8, tok), 1) + base
    pos_row = lax.broadcasted_iota(jnp.int32, (tok, HD), 0) + base
    start_row = jnp.zeros((8, tok), jnp.int32)
    w_row = jnp.zeros((8, tok), f32)
    w_col = jnp.zeros((tok, HD), f32)
    for d in range(docs):
        start_row = jnp.where(pos_lane >= starts[d], starts[d], start_row)
        w_row = jnp.where(pos_lane >= starts[d], weights[d], w_row)
        w_col = jnp.where(pos_row >= starts[d], weights[d], w_col)
    wcol[...] = w_col * (-SCALE)
    w_row = w_row[0:1] * SCALE
    query_pos = lax.broadcasted_iota(jnp.int32, (tok, tok), 1) + base
    for i, behind in enumerate((0, 2, 4, 1, 3)):
        key_pos = lax.broadcasted_iota(jnp.int32, (tok, tok), 0) + (base - behind * tok)
        allowed = (key_pos >= start_row[0:1]) & (key_pos <= query_pos)
        bias[i * tok : (i + 1) * tok, :] = jnp.where(allowed, 0.0, -1e30).astype(f32)
    load_small(2).wait()
    norm_t[...] = norm_s[...] * LOG2E
    lane = lax.broadcasted_iota(jnp.int32, (tok, HD), 1)

    def row_deltas(g):
        load(g, 1).wait()
        load(g, 2).wait()
        delta = jnp.zeros((tok, HD), f32)
        for h in range(GQA):
            cols = slice(h * HD, (h + 1) * HD)
            prod = do_s[g, :, cols].astype(f32) * o_s[g, :, cols].astype(f32)
            delta = jnp.where(lane == h, jnp.sum(prod, axis=1, keepdims=True), delta)
        delta_t[pl.ds(pl.multiple_of(g * GQA, GQA), GQA), :] = delta.T[0:GQA]

    each(0, KVH, row_deltas)
    each(0, KVH, lambda g: load(g, 0).wait())

    def pass_on(u):
        near(u).wait_recv()
        far(u).start()

    def give_mate(u):
        far(u).wait_recv()
        share(u).start()

    def put_grad(u, block):
        pair_out[u] = block[3 * tok :].astype(bf16)
        pair(u).start()
        own[u] = block[0 : 3 * tok]

    def stack(ref, g):
        return jnp.concatenate([ref[g, :, h * HD : (h + 1) * HD] for h in range(GQA)], 0)

    def probs_phase(g):
        keys = kv[2 * g]
        norm = norm_t[pl.ds(pl.multiple_of(g * GQA, GQA), GQA), :]
        mask = bias[...]
        for h in range(GQA):
            cols = slice(h * HD, (h + 1) * HD)
            if h % 2 == 0:
                two = jnp.concatenate([q_s[g, :, cols], q_s[g, :, (h + 1) * HD : (h + 2) * HD]], 0)
                both = lax.dot_general(keys, two, NT, preferred_element_type=f32)
            s = both[:, (h % 2) * HD : (h % 2 + 1) * HD]
            p = jnp.exp2(s * (SCALE * LOG2E) + mask - norm[h : h + 1])
            mean_t[h : h + 1, :] = jnp.sum(p * s, axis=0, keepdims=True)
            p32_s[:, cols] = p
            p_s[:, cols] = p.astype(bf16)
        put_grad(2 * g, jnp.dot(p_s[...], stack(do_s, g), preferred_element_type=f32))

    def grads_phase(g):
        window = jnp.concatenate([kv[2 * g], kv[2 * g + 1]], 1)
        delta = delta_t[pl.ds(pl.multiple_of(g * GQA, GQA), GQA), :]
        offset = w_row * mean_t[...] - delta
        for h in range(GQA):
            cols = slice(h * HD, (h + 1) * HD)
            if h % 2 == 0:
                sides = [
                    jnp.concatenate([(q_s[g, :, c].astype(f32) * wcol[...]).astype(bf16), do_s[g, :, c]], 1)
                    for c in (cols, slice((h + 1) * HD, (h + 2) * HD))
                ]
                both = lax.dot_general(window, jnp.concatenate(sides, 0), NT, preferred_element_type=f32)
            gs = both[:, (h % 2) * HD : (h % 2 + 1) * HD]
            ds_s[g, :, cols] = (p32_s[:, cols] * (gs + offset[h : h + 1])).astype(bf16)
        put_grad(
            2 * g + 1, jnp.dot(ds_s[g], stack(q_s, g), preferred_element_type=f32) * SCALE
        )

    def query_phase(g):
        dq_t = jnp.dot(kv[2 * g].T, ds_s[g], preferred_element_type=f32) * SCALE
        for h in range(GQA):
            cols = slice(h * HD, (h + 1) * HD)
            dq_ref[g, :, cols] = dq_t[:, cols].T.astype(bf16)

    def grads_mate(u):
        pair(u).wait_recv()
        one = pair_in[u, 0:tok].astype(f32)
        three = pair_in[u, tok:].astype(f32)
        zero = jnp.zeros_like(one)
        far_out[u] = (own[u, 2 * tok :] + jnp.where(even, zero, three)).astype(bf16)
        own[u, 0:tok] = own[u, 0:tok] + jnp.where(even, one, zero)
        return own[u, tok : 2 * tok] + jnp.where(even, three, one)

    def grads_mate_pass(u):
        block = grads_mate(u)
        back_far(u).start()
        own[u, tok : 2 * tok] = block

    def grads_mate_straight(u):
        block = grads_mate(u)
        back_far_two(u).start()
        near_out[u] = block.astype(bf16)
        back_near(u).start()

    def grads_pass(u):
        back_far(u).wait_recv()
        near_out[u] = (own[u, tok : 2 * tok] + far_in[u].astype(f32)).astype(bf16)
        back_near(u).start()

    def last(u):
        @pl.when((u < STRAIGHT_FIRST) | (u >= units - STRAIGHT_LAST))
        def _():
            back_far_two(u).wait_recv()
            own[u, 0:tok] = own[u, 0:tok] + far_in[u].astype(f32)

        back_near(u).wait_recv()
        total = (own[u, 0:tok] + near_in[u].astype(f32)).astype(bf16)
        cols = pl.ds(pl.multiple_of((u // 2) * HD, HD), HD)

        @pl.when(u % 2 == 0)
        def _():
            dv_ref[:, cols] = total

        @pl.when(u % 2 == 1)
        def _():
            dk_ref[:, cols] = total

    def merge(u):
        straight = ((u >= 0) & (u < STRAIGHT_FIRST)) | (u >= units - STRAIGHT_LAST)
        pl.when(straight)(lambda: grads_mate_straight(u))
        pl.when((u >= 0) & jnp.logical_not(straight))(lambda: grads_mate_pass(u))

    def between(u):
        merge(u - 1)

        @pl.when(u + AHEAD_PASS < units)
        def _():
            pass_on(u + AHEAD_PASS)

        @pl.when(u + AHEAD_SEND < units)
        def _():
            near(u + AHEAD_SEND).start()

        @pl.when(u + AHEAD_PAIR < units)
        def _():
            give_mate(u + AHEAD_PAIR)

        @pl.when(u >= LAG_PASS + STRAIGHT_FIRST)
        def _():
            grads_pass(u - LAG_PASS)

        @pl.when(u >= LAG_LAST)
        def _():
            last(u - LAG_LAST)

    for u in range(AHEAD_PASS):
        pass_on(u)
        if AHEAD_PASS + u < AHEAD_SEND:
            near(AHEAD_PASS + u).start()
    for u in range(2 * AHEAD_PASS, AHEAD_SEND):
        near(u).start()
    for u in range(AHEAD_PAIR):
        give_mate(u)

    def step(g, carry):
        share(2 * g).wait_recv()
        probs_phase(g)
        between(2 * g)
        share(2 * g + 1).wait_recv()
        grads_phase(g)
        between(2 * g + 1)
        return carry

    lax.fori_loop(0, KVH, step, 0)
    merge(units - 1)
    each(units - LAG_PASS, units - STRAIGHT_LAST, grads_pass)
    each(0, KVH, query_phase)

    def sent(u):
        for copy in (near, far, share, pair, back_far):
            copy(u).wait_send()

    each(0, units, sent)
    each(0, units - STRAIGHT_LAST, lambda u: back_near(u).wait_send())
    each(units - LAG_LAST, units, last)
    each(units - STRAIGHT_LAST, units, lambda u: back_near(u).wait_send())


def out_kernel(dq_in, dk_in, dv_in, dq, dk, dv, sems):
    groups = dq_in.shape[0]
    copies = [
        pltpu.make_async_copy(dq_in.at[g], dq.at[:, g * GW : (g + 1) * GW], sems.at[g])
        for g in range(groups)
    ]
    copies.append(pltpu.make_async_copy(dk_in, dk, sems.at[groups]))
    copies.append(pltpu.make_async_copy(dv_in, dv, sems.at[groups + 1]))
    for copy in copies:
        copy.start()
    for copy in copies:
        copy.wait()


def finish_out(dq, dk, dv):
    vmem = pl.BlockSpec(memory_space=pltpu.VMEM)
    hbm = pl.BlockSpec(memory_space=pl.ANY)
    groups, tok, width = dq.shape
    return pl.pallas_call(
        out_kernel,
        out_shape=(
            jax.ShapeDtypeStruct((tok, groups * width), dq.dtype),
            jax.ShapeDtypeStruct(dk.shape, dk.dtype),
            jax.ShapeDtypeStruct(dv.shape, dv.dtype),
        ),
        in_specs=[vmem] * 3,
        out_specs=(hbm,) * 3,
        scratch_shapes=[pltpu.SemaphoreType.DMA((groups + 2,))],
        compiler_params=pltpu.CompilerParams(vmem_limit_bytes=VMEM_BYTES),
    )(dq, dk, dv)


def per_device(
    queries, key_rows, value_rows, outputs, out_grads, log_normalizer, doc_starts, doc_weights
):
    tok = queries.shape[0]
    units = 2 * KVH
    vmem = pl.BlockSpec(memory_space=pltpu.VMEM)
    smem = pl.BlockSpec(memory_space=pltpu.SMEM)
    hbm = pl.BlockSpec(memory_space=pl.ANY)
    dma = pltpu.SemaphoreType.DMA
    heads = pltpu.VMEM((KVH, tok, GW), bf16)
    block = pltpu.VMEM((units, tok, HD), bf16)
    pair = pltpu.VMEM((units, 2 * tok, HD), bf16)
    tile = pltpu.VMEM((5 * tok, GW), bf16)
    out = pl.pallas_call(
        kernel,
        out_shape=(
            pltpu.VMEM((KVH, tok, GW), bf16),
            pltpu.VMEM(key_rows.shape, bf16),
            pltpu.VMEM(value_rows.shape, bf16),
        ),
        in_specs=[smem, smem] + [hbm] * 6,
        out_specs=(vmem,) * 3,
        scratch_shapes=[
            pltpu.VMEM((units, 5 * tok, HD), bf16),
            heads, heads, heads,
            pltpu.VMEM((5 * tok, tok), f32),
            pltpu.VMEM((tok, HD), f32),
            pltpu.VMEM((HEADS, tok), f32),
            pltpu.VMEM((HEADS, tok), f32),
            pltpu.VMEM((GQA, tok), f32),
            pltpu.VMEM((5 * tok, GW), f32),
            tile,
            pltpu.VMEM((KVH, 5 * tok, GW), bf16),
            pltpu.VMEM(key_rows.shape, bf16),
            pltpu.VMEM(value_rows.shape, bf16),
            pltpu.VMEM((HEADS, tok), f32),
            pair, pair,
            pltpu.VMEM((units, 3 * tok, HD), f32),
            block, block, block, block,
            dma((3, KVH)),
            dma((3,)),
        ]
        + [dma((2, units))] * 6,
        compiler_params=pltpu.CompilerParams(
            collective_id=0, has_side_effects=True, vmem_limit_bytes=VMEM_BYTES
        ),
        cost_estimate=pl.CostEstimate(
            flops=10 * HEADS * tok * 5 * tok * HD, bytes_accessed=9 * queries.size, transcendentals=0
        ),
    )(doc_starts, doc_weights, queries, out_grads, outputs, key_rows, value_rows, log_normalizer.T)
    return finish_out(*[pltpu.with_memory_space_constraint(x, pltpu.VMEM) for x in out])


def solution(mesh):
    rows = P(("dp", "seq"), None)
    in_specs = (rows, rows, rows, rows, rows, rows, P("dp"), P("dp"))
    return jax.shard_map(
        per_device, mesh=mesh, in_specs=in_specs, out_specs=(rows, rows, rows), check_vma=False
    )
```

```python
import functools
import math

import jax
import jax.numpy as jnp
from jax import lax
from jax.experimental import pallas as pl
from jax.experimental.pallas import tpu as pltpu
from jax.sharding import PartitionSpec as P

HEADS = 64
KVH = 8
HD = 128
GQA = HEADS // KVH
GW = GQA * HD
SCALE = HD ** (-0.5)
LOG2E = math.log2(math.e)
NT = (((1,), (1,)), ((), ()))
VMEM_BYTES = 56 * 1024 * 1024
f32 = jnp.float32
bf16 = jnp.bfloat16

AHEAD_SEND = 8
AHEAD_PASS = 5
AHEAD_PAIR = 2
LAG_PASS = 4
LAG_LAST = 7
STRAIGHT_FIRST = 0
STRAIGHT_LAST = 1
GREET_TWO = 10


def kernel(
    starts, weights, q_hbm, do_hbm, o_hbm, k_hbm, v_hbm, norm_hbm,
    dq_ref, dk_ref, dv_ref,
    kv, q_s, do_s, o_s, bias, wcol, norm_t, delta_t, mean_t, p32_s, p_s, ds_s, k_s, v_s, norm_s,
    pair_out, pair_in, own, far_out, far_in, near_out, near_in,
    in_sem, small_sem, near_sem, far_sem, mate_sem, pair_sem, back_far_sem, back_near_sem,
):
    tok = k_hbm.shape[0]
    docs = starts.shape[0]
    units = 2 * KVH
    me = lax.axis_index("seq")
    n = lax.axis_size("seq")
    parity = lax.rem(me, 2)
    even = parity == 0
    up = {"seq": lax.rem(me + 2, n)}
    up_two = {"seq": lax.rem(me + 4, n)}
    down = {"seq": lax.rem(me + n - 2, n)}
    down_two = {"seq": lax.rem(me + n - 4, n)}
    mate = {"seq": me + 1 - 2 * parity}

    def load(g, i):
        src = (q_hbm, do_hbm, o_hbm)[i]
        dst = (q_s, do_s, o_s)[i]
        return pltpu.make_async_copy(
            src.at[:, pl.ds(pl.multiple_of(g * GW, GW), GW)], dst.at[g], in_sem.at[i, g]
        )

    def load_small(i):
        src = (k_hbm, v_hbm, norm_hbm)[i]
        dst = (k_s, v_s, norm_s)[i]
        return pltpu.make_async_copy(src, dst, small_sem.at[i])

    def remote(src, dst, sem, u, where):
        return pltpu.make_async_remote_copy(
            src_ref=src, dst_ref=dst, send_sem=sem.at[0, u], recv_sem=sem.at[1, u],
            device_id=where, device_id_type=pl.DeviceIdType.MESH,
        )

    def rows(u, start, size=1):
        return kv.at[u, pl.ds(start, size * tok), :]

    def near(u):
        return remote(rows(u, 0), rows(u, tok), near_sem, u, up)

    def far(u):
        return remote(rows(u, tok), rows(u, 2 * tok), far_sem, u, up)

    def share(u):
        src = pl.multiple_of(parity * tok, tok)
        return remote(rows(u, src, 2), rows(u, 3 * tok, 2), mate_sem, u, mate)

    def pair(u):
        return remote(pair_out.at[u], pair_in.at[u], pair_sem, u, mate)

    def back_far(u):
        return remote(far_out.at[u], far_in.at[u], back_far_sem, u, down)

    def back_far_two(u):
        return remote(far_out.at[u], far_in.at[u], back_far_sem, u, down_two)

    def back_near(u):
        return remote(near_out.at[u], near_in.at[u], back_near_sem, u, down)

    def each(lo, hi, fn):
        def step(i, carry):
            fn(i)
            return carry
        lax.fori_loop(lo, hi, step, 0)

    barrier = pltpu.get_barrier_semaphore()

    def greet(partners):
        for where in partners:
            pl.semaphore_signal(barrier, inc=1, device_id=where, device_id_type=pl.DeviceIdType.MESH)

    greet((up, down, mate))
    for i in range(3):
        load_small(i).start()
    for i in (1, 2, 0):
        each(0, KVH, lambda g: load(g, i).start())
    load_small(0).wait()
    load_small(1).wait()
    for g in range(KVH):
        kv[2 * g, 0:tok, :] = k_s[:, g * HD : (g + 1) * HD]
        kv[2 * g + 1, 0:tok, :] = v_s[:, g * HD : (g + 1) * HD]
    pl.semaphore_wait(barrier, 3)
    for u in range(AHEAD_PASS):
        near(u).start()

    base = me * tok
    pos_lane = lax.broadcasted_iota(jnp.int32, (8, tok), 1) + base
    pos_row = lax.broadcasted_iota(jnp.int32, (tok, HD), 0) + base
    start_row = jnp.zeros((8, tok), jnp.int32)
    w_row = jnp.zeros((8, tok), f32)
    w_col = jnp.zeros((tok, HD), f32)
    for d in range(docs):
        start_row = jnp.where(pos_lane >= starts[d], starts[d], start_row)
        w_row = jnp.where(pos_lane >= starts[d], weights[d], w_row)
        w_col = jnp.where(pos_row >= starts[d], weights[d], w_col)
    wcol[...] = w_col * (-SCALE)
    w_row = w_row[0:1] * SCALE
    query_pos = lax.broadcasted_iota(jnp.int32, (tok, tok), 1) + base
    for i, behind in enumerate((0, 2, 4, 1, 3)):
        key_pos = lax.broadcasted_iota(jnp.int32, (tok, tok), 0) + (base - behind * tok)
        allowed = (key_pos >= start_row[0:1]) & (key_pos <= query_pos)
        bias[i * tok : (i + 1) * tok, :] = jnp.where(allowed, 0.0, -1e30).astype(f32)
    load_small(2).wait()
    norm_t[...] = norm_s[...] * LOG2E
    lane = lax.broadcasted_iota(jnp.int32, (tok, HD), 1)

    def row_deltas(g):
        load(g, 1).wait()
        load(g, 2).wait()
        delta = jnp.zeros((tok, HD), f32)
        for h in range(GQA):
            cols = slice(h * HD, (h + 1) * HD)
            prod = do_s[g, :, cols].astype(f32) * o_s[g, :, cols].astype(f32)
            delta = jnp.where(lane == h, jnp.sum(prod, axis=1, keepdims=True), delta)
        delta_t[pl.ds(pl.multiple_of(g * GQA, GQA), GQA), :] = delta.T[0:GQA]

    each(0, KVH, row_deltas)
    each(0, KVH, lambda g: load(g, 0).wait())

    def pass_on(u):
        near(u).wait_recv()
        far(u).start()

    def give_mate(u):
        far(u).wait_recv()
        share(u).start()

    def put_grad(u, block):
        pair_out[u] = block[3 * tok :].astype(bf16)
        pair(u).start()
        own[u] = block[0 : 3 * tok]

    def stack(ref, g):
        return jnp.concatenate([ref[g, :, h * HD : (h + 1) * HD] for h in range(GQA)], 0)

    def probs_phase(g):
        keys = kv[2 * g]
        norm = norm_t[pl.ds(pl.multiple_of(g * GQA, GQA), GQA), :]
        mask = bias[...]
        for h in range(GQA):
            cols = slice(h * HD, (h + 1) * HD)
            if h % 2 == 0:
                two = jnp.concatenate([q_s[g, :, cols], q_s[g, :, (h + 1) * HD : (h + 2) * HD]], 0)
                both = lax.dot_general(keys, two, NT, preferred_element_type=f32)
            s = both[:, (h % 2) * HD : (h % 2 + 1) * HD]
            p = jnp.exp2(s * (SCALE * LOG2E) + mask - norm[h : h + 1])
            mean_t[h : h + 1, :] = jnp.sum(p * s, axis=0, keepdims=True)
            p32_s[:, cols] = p
            p_s[:, cols] = p.astype(bf16)
        put_grad(2 * g, jnp.dot(p_s[...], stack(do_s, g), preferred_element_type=f32))

    def grads_phase(g):
        window = jnp.concatenate([kv[2 * g], kv[2 * g + 1]], 1)
        delta = delta_t[pl.ds(pl.multiple_of(g * GQA, GQA), GQA), :]
        offset = w_row * mean_t[...] - delta
        for h in range(GQA):
            cols = slice(h * HD, (h + 1) * HD)
            if h % 2 == 0:
                sides = [
                    jnp.concatenate([(q_s[g, :, c].astype(f32) * wcol[...]).astype(bf16), do_s[g, :, c]], 1)
                    for c in (cols, slice((h + 1) * HD, (h + 2) * HD))
                ]
                both = lax.dot_general(window, jnp.concatenate(sides, 0), NT, preferred_element_type=f32)
            gs = both[:, (h % 2) * HD : (h % 2 + 1) * HD]
            ds_s[g, :, cols] = (p32_s[:, cols] * (gs + offset[h : h + 1])).astype(bf16)
        put_grad(
            2 * g + 1, jnp.dot(ds_s[g], stack(q_s, g), preferred_element_type=f32) * SCALE
        )

    def query_phase(g):
        dq_t = jnp.dot(kv[2 * g].T, ds_s[g], preferred_element_type=f32) * SCALE
        for h in range(GQA):
            cols = slice(h * HD, (h + 1) * HD)
            dq_ref[g, :, cols] = dq_t[:, cols].T.astype(bf16)

    def grads_mate(u):
        pair(u).wait_recv()
        one = pair_in[u, 0:tok].astype(f32)
        three = pair_in[u, tok:].astype(f32)
        zero = jnp.zeros_like(one)
        far_out[u] = (own[u, 2 * tok :] + jnp.where(even, zero, three)).astype(bf16)
        own[u, 0:tok] = own[u, 0:tok] + jnp.where(even, one, zero)
        return own[u, tok : 2 * tok] + jnp.where(even, three, one)

    def grads_mate_pass(u):
        block = grads_mate(u)
        back_far(u).start()
        own[u, tok : 2 * tok] = block

    def grads_mate_straight(u):
        block = grads_mate(u)
        back_far_two(u).start()
        near_out[u] = block.astype(bf16)
        back_near(u).start()

    def grads_pass(u):
        back_far(u).wait_recv()
        near_out[u] = (own[u, tok : 2 * tok] + far_in[u].astype(f32)).astype(bf16)
        back_near(u).start()

    def last(u):
        @pl.when((u < STRAIGHT_FIRST) | (u >= units - STRAIGHT_LAST))
        def _():
            back_far_two(u).wait_recv()
            own[u, 0:tok] = own[u, 0:tok] + far_in[u].astype(f32)

        back_near(u).wait_recv()
        total = (own[u, 0:tok] + near_in[u].astype(f32)).astype(bf16)
        cols = pl.ds(pl.multiple_of((u // 2) * HD, HD), HD)

        @pl.when(u % 2 == 0)
        def _():
            dv_ref[:, cols] = total

        @pl.when(u % 2 == 1)
        def _():
            dk_ref[:, cols] = total

    def merge(u):
        straight = ((u >= 0) & (u < STRAIGHT_FIRST)) | (u >= units - STRAIGHT_LAST)
        pl.when(straight)(lambda: grads_mate_straight(u))
        pl.when((u >= 0) & jnp.logical_not(straight))(lambda: grads_mate_pass(u))

    def between(u):
        merge(u - 1)

        @pl.when(u + AHEAD_PASS < units)
        def _():
            pass_on(u + AHEAD_PASS)

        @pl.when(u + AHEAD_SEND < units)
        def _():
            near(u + AHEAD_SEND).start()

        @pl.when(u + AHEAD_PAIR < units)
        def _():
            give_mate(u + AHEAD_PAIR)

        @pl.when(u >= LAG_PASS + STRAIGHT_FIRST)
        def _():
            grads_pass(u - LAG_PASS)

        @pl.when(u >= LAG_LAST)
        def _():
            last(u - LAG_LAST)

        @pl.when(u == GREET_TWO)
        def _():
            greet((up_two, down_two))

    for u in range(AHEAD_PASS):
        pass_on(u)
        if AHEAD_PASS + u < AHEAD_SEND:
            near(AHEAD_PASS + u).start()
    for u in range(2 * AHEAD_PASS, AHEAD_SEND):
        near(u).start()
    for u in range(AHEAD_PAIR):
        give_mate(u)

    def step(g, carry):
        share(2 * g).wait_recv()
        probs_phase(g)
        between(2 * g)
        share(2 * g + 1).wait_recv()
        grads_phase(g)
        between(2 * g + 1)
        return carry

    lax.fori_loop(0, KVH, step, 0)
    pl.semaphore_wait(barrier, 2)
    merge(units - 1)
    each(units - LAG_PASS, units - STRAIGHT_LAST, grads_pass)
    each(0, KVH, query_phase)

    def sent(u):
        for copy in (near, far, share, pair, back_far):
            copy(u).wait_send()

    each(0, units, sent)
    each(0, units - STRAIGHT_LAST, lambda u: back_near(u).wait_send())
    each(units - LAG_LAST, units, last)
    each(units - STRAIGHT_LAST, units, lambda u: back_near(u).wait_send())


def out_kernel(dq_in, dk_in, dv_in, dq, dk, dv, sems):
    groups = dq_in.shape[0]
    copies = [
        pltpu.make_async_copy(dq_in.at[g], dq.at[:, g * GW : (g + 1) * GW], sems.at[g])
        for g in range(groups)
    ]
    copies.append(pltpu.make_async_copy(dk_in, dk, sems.at[groups]))
    copies.append(pltpu.make_async_copy(dv_in, dv, sems.at[groups + 1]))
    for copy in copies:
        copy.start()
    for copy in copies:
        copy.wait()


def finish_out(dq, dk, dv):
    vmem = pl.BlockSpec(memory_space=pltpu.VMEM)
    hbm = pl.BlockSpec(memory_space=pl.ANY)
    groups, tok, width = dq.shape
    return pl.pallas_call(
        out_kernel,
        out_shape=(
            jax.ShapeDtypeStruct((tok, groups * width), dq.dtype),
            jax.ShapeDtypeStruct(dk.shape, dk.dtype),
            jax.ShapeDtypeStruct(dv.shape, dv.dtype),
        ),
        in_specs=[vmem] * 3,
        out_specs=(hbm,) * 3,
        scratch_shapes=[pltpu.SemaphoreType.DMA((groups + 2,))],
        compiler_params=pltpu.CompilerParams(vmem_limit_bytes=VMEM_BYTES),
    )(dq, dk, dv)


def per_device(
    queries, key_rows, value_rows, outputs, out_grads, log_normalizer, doc_starts, doc_weights
):
    tok = queries.shape[0]
    units = 2 * KVH
    vmem = pl.BlockSpec(memory_space=pltpu.VMEM)
    smem = pl.BlockSpec(memory_space=pltpu.SMEM)
    hbm = pl.BlockSpec(memory_space=pl.ANY)
    dma = pltpu.SemaphoreType.DMA
    heads = pltpu.VMEM((KVH, tok, GW), bf16)
    block = pltpu.VMEM((units, tok, HD), bf16)
    pair = pltpu.VMEM((units, 2 * tok, HD), bf16)
    tile = pltpu.VMEM((5 * tok, GW), bf16)
    out = pl.pallas_call(
        kernel,
        out_shape=(
            pltpu.VMEM((KVH, tok, GW), bf16),
            pltpu.VMEM(key_rows.shape, bf16),
            pltpu.VMEM(value_rows.shape, bf16),
        ),
        in_specs=[smem, smem] + [hbm] * 6,
        out_specs=(vmem,) * 3,
        scratch_shapes=[
            pltpu.VMEM((units, 5 * tok, HD), bf16),
            heads, heads, heads,
            pltpu.VMEM((5 * tok, tok), f32),
            pltpu.VMEM((tok, HD), f32),
            pltpu.VMEM((HEADS, tok), f32),
            pltpu.VMEM((HEADS, tok), f32),
            pltpu.VMEM((GQA, tok), f32),
            pltpu.VMEM((5 * tok, GW), f32),
            tile,
            pltpu.VMEM((KVH, 5 * tok, GW), bf16),
            pltpu.VMEM(key_rows.shape, bf16),
            pltpu.VMEM(value_rows.shape, bf16),
            pltpu.VMEM((HEADS, tok), f32),
            pair, pair,
            pltpu.VMEM((units, 3 * tok, HD), f32),
            block, block, block, block,
            dma((3, KVH)),
            dma((3,)),
        ]
        + [dma((2, units))] * 6,
        compiler_params=pltpu.CompilerParams(
            collective_id=0, has_side_effects=True, vmem_limit_bytes=VMEM_BYTES
        ),
        cost_estimate=pl.CostEstimate(
            flops=10 * HEADS * tok * 5 * tok * HD, bytes_accessed=9 * queries.size, transcendentals=0
        ),
    )(doc_starts, doc_weights, queries, out_grads, outputs, key_rows, value_rows, log_normalizer.T)
    return finish_out(*[pltpu.with_memory_space_constraint(x, pltpu.VMEM) for x in out])


def solution(mesh):
    rows = P(("dp", "seq"), None)
    in_specs = (rows, rows, rows, rows, rows, rows, P("dp"), P("dp"))
    return jax.shard_map(
        per_device, mesh=mesh, in_specs=in_specs, out_specs=(rows, rows, rows), check_vma=False
    )
```

```python
import functools
import math

import jax
import jax.numpy as jnp
from jax import lax
from jax.experimental import pallas as pl
from jax.experimental.pallas import tpu as pltpu
from jax.sharding import PartitionSpec as P

HEADS = 64
KVH = 8
HD = 128
GQA = HEADS // KVH
GW = GQA * HD
SCALE = HD ** (-0.5)
LOG2E = math.log2(math.e)
NT = (((1,), (1,)), ((), ()))
VMEM_BYTES = 56 * 1024 * 1024
f32 = jnp.float32
bf16 = jnp.bfloat16

AHEAD_SEND = 8
AHEAD_PASS = 5
AHEAD_PAIR = 2
LAG_PASS = 4
LAG_LAST = 8
STRAIGHT_FIRST = 0
STRAIGHT_LAST = 1
GREET_TWO = 10


def kernel(
    starts, weights, q_hbm, do_hbm, o_hbm, k_hbm, v_hbm, norm_hbm,
    dq_ref, dk_ref, dv_ref,
    kv, q_s, do_s, o_s, bias, wcol, norm_t, delta_t, mean_t, p32_s, p_s, ds_s, k_s, v_s, norm_s,
    pair_out, pair_in, own, far_out, far_in, near_out, near_in,
    in_sem, small_sem, near_sem, far_sem, mate_sem, pair_sem, back_far_sem, back_near_sem,
):
    tok = k_hbm.shape[0]
    docs = starts.shape[0]
    units = 2 * KVH
    me = lax.axis_index("seq")
    n = lax.axis_size("seq")
    parity = lax.rem(me, 2)
    even = parity == 0
    up = {"seq": lax.rem(me + 2, n)}
    up_two = {"seq": lax.rem(me + 4, n)}
    down = {"seq": lax.rem(me + n - 2, n)}
    down_two = {"seq": lax.rem(me + n - 4, n)}
    mate = {"seq": me + 1 - 2 * parity}

    def load(g, i):
        src = (q_hbm, do_hbm, o_hbm)[i]
        dst = (q_s, do_s, o_s)[i]
        return pltpu.make_async_copy(
            src.at[:, pl.ds(pl.multiple_of(g * GW, GW), GW)], dst.at[g], in_sem.at[i, g]
        )

    def load_small(i):
        src = (k_hbm, v_hbm, norm_hbm)[i]
        dst = (k_s, v_s, norm_s)[i]
        return pltpu.make_async_copy(src, dst, small_sem.at[i])

    def remote(src, dst, sem, u, where):
        return pltpu.make_async_remote_copy(
            src_ref=src, dst_ref=dst, send_sem=sem.at[0, u], recv_sem=sem.at[1, u],
            device_id=where, device_id_type=pl.DeviceIdType.MESH,
        )

    def rows(u, start, size=1):
        return kv.at[u, pl.ds(start, size * tok), :]

    def near(u):
        return remote(rows(u, 0), rows(u, tok), near_sem, u, up)

    def far(u):
        return remote(rows(u, tok), rows(u, 2 * tok), far_sem, u, up)

    def share(u):
        src = pl.multiple_of(parity * tok, tok)
        return remote(rows(u, src, 2), rows(u, 3 * tok, 2), mate_sem, u, mate)

    def pair(u):
        return remote(pair_out.at[u], pair_in.at[u], pair_sem, u, mate)

    def back_far(u):
        return remote(far_out.at[u], far_in.at[u], back_far_sem, u, down)

    def back_far_two(u):
        return remote(far_out.at[u], far_in.at[u], back_far_sem, u, down_two)

    def back_near(u):
        return remote(near_out.at[u], near_in.at[u], back_near_sem, u, down)

    def each(lo, hi, fn):
        def step(i, carry):
            fn(i)
            return carry
        lax.fori_loop(lo, hi, step, 0)

    barrier = pltpu.get_barrier_semaphore()

    def greet(partners):
        for where in partners:
            pl.semaphore_signal(barrier, inc=1, device_id=where, device_id_type=pl.DeviceIdType.MESH)

    greet((up, down, mate))
    for i in range(3):
        load_small(i).start()
    for i in (1, 2, 0):
        each(0, KVH, lambda g: load(g, i).start())
    load_small(0).wait()
    load_small(1).wait()
    for g in range(KVH):
        kv[2 * g, 0:tok, :] = k_s[:, g * HD : (g + 1) * HD]
        kv[2 * g + 1, 0:tok, :] = v_s[:, g * HD : (g + 1) * HD]
    pl.semaphore_wait(barrier, 3)
    for u in range(AHEAD_PASS):
        near(u).start()

    base = me * tok
    pos_lane = lax.broadcasted_iota(jnp.int32, (8, tok), 1) + base
    pos_row = lax.broadcasted_iota(jnp.int32, (tok, HD), 0) + base
    start_row = jnp.zeros((8, tok), jnp.int32)
    w_row = jnp.zeros((8, tok), f32)
    w_col = jnp.zeros((tok, HD), f32)
    for d in range(docs):
        start_row = jnp.where(pos_lane >= starts[d], starts[d], start_row)
        w_row = jnp.where(pos_lane >= starts[d], weights[d], w_row)
        w_col = jnp.where(pos_row >= starts[d], weights[d], w_col)
    wcol[...] = w_col * (-SCALE)
    w_row = w_row[0:1] * SCALE
    query_pos = lax.broadcasted_iota(jnp.int32, (tok, tok), 1) + base
    for i, behind in enumerate((0, 2, 4, 1, 3)):
        key_pos = lax.broadcasted_iota(jnp.int32, (tok, tok), 0) + (base - behind * tok)
        allowed = (key_pos >= start_row[0:1]) & (key_pos <= query_pos)
        bias[i * tok : (i + 1) * tok, :] = jnp.where(allowed, 0.0, -1e30).astype(f32)
    load_small(2).wait()
    norm_t[...] = norm_s[...] * LOG2E
    lane = lax.broadcasted_iota(jnp.int32, (tok, HD), 1)

    def row_deltas(g):
        load(g, 1).wait()
        load(g, 2).wait()
        delta = jnp.zeros((tok, HD), f32)
        for h in range(GQA):
            cols = slice(h * HD, (h + 1) * HD)
            prod = do_s[g, :, cols].astype(f32) * o_s[g, :, cols].astype(f32)
            delta = jnp.where(lane == h, jnp.sum(prod, axis=1, keepdims=True), delta)
        delta_t[pl.ds(pl.multiple_of(g * GQA, GQA), GQA), :] = delta.T[0:GQA]

    each(0, KVH, row_deltas)
    each(0, KVH, lambda g: load(g, 0).wait())

    def pass_on(u):
        near(u).wait_recv()
        far(u).start()

    def give_mate(u):
        far(u).wait_recv()
        share(u).start()

    def put_grad(u, block):
        pair_out[u] = block[3 * tok :].astype(bf16)
        pair(u).start()
        own[u] = block[0 : 3 * tok]

    def stack(ref, g):
        return jnp.concatenate([ref[g, :, h * HD : (h + 1) * HD] for h in range(GQA)], 0)

    def probs_phase(g):
        keys = kv[2 * g]
        norm = norm_t[pl.ds(pl.multiple_of(g * GQA, GQA), GQA), :]
        mask = bias[...]
        for h in range(GQA):
            cols = slice(h * HD, (h + 1) * HD)
            if h % 2 == 0:
                two = jnp.concatenate([q_s[g, :, cols], q_s[g, :, (h + 1) * HD : (h + 2) * HD]], 0)
                both = lax.dot_general(keys, two, NT, preferred_element_type=f32)
            s = both[:, (h % 2) * HD : (h % 2 + 1) * HD]
            p = jnp.exp2(s * (SCALE * LOG2E) + mask - norm[h : h + 1])
            mean_t[h : h + 1, :] = jnp.sum(p * s, axis=0, keepdims=True)
            p32_s[:, cols] = p
            p_s[:, cols] = p.astype(bf16)
        put_grad(2 * g, jnp.dot(p_s[...], stack(do_s, g), preferred_element_type=f32))

    def grads_phase(g):
        window = jnp.concatenate([kv[2 * g], kv[2 * g + 1]], 1)
        delta = delta_t[pl.ds(pl.multiple_of(g * GQA, GQA), GQA), :]
        offset = w_row * mean_t[...] - delta
        for h in range(GQA):
            cols = slice(h * HD, (h + 1) * HD)
            if h % 2 == 0:
                sides = [
                    jnp.concatenate([(q_s[g, :, c].astype(f32) * wcol[...]).astype(bf16), do_s[g, :, c]], 1)
                    for c in (cols, slice((h + 1) * HD, (h + 2) * HD))
                ]
                both = lax.dot_general(window, jnp.concatenate(sides, 0), NT, preferred_element_type=f32)
            gs = both[:, (h % 2) * HD : (h % 2 + 1) * HD]
            ds_s[g, :, cols] = (p32_s[:, cols] * (gs + offset[h : h + 1])).astype(bf16)
        put_grad(
            2 * g + 1, jnp.dot(ds_s[g], stack(q_s, g), preferred_element_type=f32) * SCALE
        )

    def query_phase(g):
        dq_t = jnp.dot(kv[2 * g].T, ds_s[g], preferred_element_type=f32) * SCALE
        for h in range(GQA):
            cols = slice(h * HD, (h + 1) * HD)
            dq_ref[g, :, cols] = dq_t[:, cols].T.astype(bf16)

    def grads_mate(u):
        pair(u).wait_recv()
        one = pair_in[u, 0:tok].astype(f32)
        three = pair_in[u, tok:].astype(f32)
        zero = jnp.zeros_like(one)
        far_out[u] = (own[u, 2 * tok :] + jnp.where(even, zero, three)).astype(bf16)
        own[u, 0:tok] = own[u, 0:tok] + jnp.where(even, one, zero)
        return own[u, tok : 2 * tok] + jnp.where(even, three, one)

    def grads_mate_pass(u):
        block = grads_mate(u)
        back_far(u).start()
        own[u, tok : 2 * tok] = block

    def grads_mate_straight(u):
        block = grads_mate(u)
        back_far_two(u).start()
        near_out[u] = block.astype(bf16)
        back_near(u).start()

    def grads_pass(u):
        back_far(u).wait_recv()
        near_out[u] = (own[u, tok : 2 * tok] + far_in[u].astype(f32)).astype(bf16)
        back_near(u).start()

    def last(u):
        @pl.when((u < STRAIGHT_FIRST) | (u >= units - STRAIGHT_LAST))
        def _():
            back_far_two(u).wait_recv()
            own[u, 0:tok] = own[u, 0:tok] + far_in[u].astype(f32)

        back_near(u).wait_recv()
        total = (own[u, 0:tok] + near_in[u].astype(f32)).astype(bf16)
        cols = pl.ds(pl.multiple_of((u // 2) * HD, HD), HD)

        @pl.when(u % 2 == 0)
        def _():
            dv_ref[:, cols] = total

        @pl.when(u % 2 == 1)
        def _():
            dk_ref[:, cols] = total

    def merge(u):
        straight = ((u >= 0) & (u < STRAIGHT_FIRST)) | (u >= units - STRAIGHT_LAST)
        pl.when(straight)(lambda: grads_mate_straight(u))
        pl.when((u >= 0) & jnp.logical_not(straight))(lambda: grads_mate_pass(u))

    def between(u):
        merge(u - 1)

        @pl.when(u + AHEAD_PASS < units)
        def _():
            pass_on(u + AHEAD_PASS)

        @pl.when(u + AHEAD_SEND < units)
        def _():
            near(u + AHEAD_SEND).start()

        @pl.when(u + AHEAD_PAIR < units)
        def _():
            give_mate(u + AHEAD_PAIR)

        @pl.when(u >= LAG_PASS + STRAIGHT_FIRST)
        def _():
            grads_pass(u - LAG_PASS)

        @pl.when(u >= LAG_LAST)
        def _():
            last(u - LAG_LAST)

        @pl.when(u == GREET_TWO)
        def _():
            greet((up_two, down_two))

    for u in range(AHEAD_PASS):
        pass_on(u)
        if AHEAD_PASS + u < AHEAD_SEND:
            near(AHEAD_PASS + u).start()
    for u in range(2 * AHEAD_PASS, AHEAD_SEND):
        near(u).start()
    for u in range(AHEAD_PAIR):
        give_mate(u)

    def step(g, carry):
        share(2 * g).wait_recv()
        probs_phase(g)
        between(2 * g)
        share(2 * g + 1).wait_recv()
        grads_phase(g)
        between(2 * g + 1)
        return carry

    lax.fori_loop(0, KVH, step, 0)
    pl.semaphore_wait(barrier, 2)
    merge(units - 1)
    each(units - LAG_PASS, units - STRAIGHT_LAST - 1, grads_pass)
    each(0, KVH // 2, query_phase)
    grads_pass(units - STRAIGHT_LAST - 1)
    each(KVH // 2, KVH, query_phase)

    def sent(u):
        for copy in (near, far, share, pair, back_far):
            copy(u).wait_send()

    each(0, units, sent)
    each(0, units - STRAIGHT_LAST, lambda u: back_near(u).wait_send())
    each(units - LAG_LAST, units, last)
    each(units - STRAIGHT_LAST, units, lambda u: back_near(u).wait_send())


def out_kernel(dq_in, dk_in, dv_in, dq, dk, dv, sems):
    groups = dq_in.shape[0]
    copies = [
        pltpu.make_async_copy(dq_in.at[g], dq.at[:, g * GW : (g + 1) * GW], sems.at[g])
        for g in range(groups)
    ]
    copies.append(pltpu.make_async_copy(dk_in, dk, sems.at[groups]))
    copies.append(pltpu.make_async_copy(dv_in, dv, sems.at[groups + 1]))
    for copy in copies:
        copy.start()
    for copy in copies:
        copy.wait()


def finish_out(dq, dk, dv):
    vmem = pl.BlockSpec(memory_space=pltpu.VMEM)
    hbm = pl.BlockSpec(memory_space=pl.ANY)
    groups, tok, width = dq.shape
    return pl.pallas_call(
        out_kernel,
        out_shape=(
            jax.ShapeDtypeStruct((tok, groups * width), dq.dtype),
            jax.ShapeDtypeStruct(dk.shape, dk.dtype),
            jax.ShapeDtypeStruct(dv.shape, dv.dtype),
        ),
        in_specs=[vmem] * 3,
        out_specs=(hbm,) * 3,
        scratch_shapes=[pltpu.SemaphoreType.DMA((groups + 2,))],
        compiler_params=pltpu.CompilerParams(vmem_limit_bytes=VMEM_BYTES),
    )(dq, dk, dv)


def per_device(
    queries, key_rows, value_rows, outputs, out_grads, log_normalizer, doc_starts, doc_weights
):
    tok = queries.shape[0]
    units = 2 * KVH
    vmem = pl.BlockSpec(memory_space=pltpu.VMEM)
    smem = pl.BlockSpec(memory_space=pltpu.SMEM)
    hbm = pl.BlockSpec(memory_space=pl.ANY)
    dma = pltpu.SemaphoreType.DMA
    heads = pltpu.VMEM((KVH, tok, GW), bf16)
    block = pltpu.VMEM((units, tok, HD), bf16)
    pair = pltpu.VMEM((units, 2 * tok, HD), bf16)
    tile = pltpu.VMEM((5 * tok, GW), bf16)
    out = pl.pallas_call(
        kernel,
        out_shape=(
            pltpu.VMEM((KVH, tok, GW), bf16),
            pltpu.VMEM(key_rows.shape, bf16),
            pltpu.VMEM(value_rows.shape, bf16),
        ),
        in_specs=[smem, smem] + [hbm] * 6,
        out_specs=(vmem,) * 3,
        scratch_shapes=[
            pltpu.VMEM((units, 5 * tok, HD), bf16),
            heads, heads, heads,
            pltpu.VMEM((5 * tok, tok), f32),
            pltpu.VMEM((tok, HD), f32),
            pltpu.VMEM((HEADS, tok), f32),
            pltpu.VMEM((HEADS, tok), f32),
            pltpu.VMEM((GQA, tok), f32),
            pltpu.VMEM((5 * tok, GW), f32),
            tile,
            pltpu.VMEM((KVH, 5 * tok, GW), bf16),
            pltpu.VMEM(key_rows.shape, bf16),
            pltpu.VMEM(value_rows.shape, bf16),
            pltpu.VMEM((HEADS, tok), f32),
            pair, pair,
            pltpu.VMEM((units, 3 * tok, HD), f32),
            block, block, block, block,
            dma((3, KVH)),
            dma((3,)),
        ]
        + [dma((2, units))] * 6,
        compiler_params=pltpu.CompilerParams(
            collective_id=0, has_side_effects=True, vmem_limit_bytes=VMEM_BYTES
        ),
        cost_estimate=pl.CostEstimate(
            flops=10 * HEADS * tok * 5 * tok * HD, bytes_accessed=9 * queries.size, transcendentals=0
        ),
    )(doc_starts, doc_weights, queries, out_grads, outputs, key_rows, value_rows, log_normalizer.T)
    return finish_out(*[pltpu.with_memory_space_constraint(x, pltpu.VMEM) for x in out])


def solution(mesh):
    rows = P(("dp", "seq"), None)
    in_specs = (rows, rows, rows, rows, rows, rows, P("dp"), P("dp"))
    return jax.shard_map(
        per_device, mesh=mesh, in_specs=in_specs, out_specs=(rows, rows, rows), check_vma=False
    )
```
